256 devices in a mesh: seq: 32 (over y, x, z_lo), resp: 8 (over z_hi, core).
Axes of the slice: x: 4, y: 4, z: 8 (z_hi: 4, z_lo: 2; z = z_hi * 2 + z_lo), core: 2. Of those that a mesh axis runs over, the one named last changes fastest.
Arguments:
- queries: bfloat16 [8, 512, 1024], P('resp', 'seq'), may hold values from -6 to 6
- grad_out: bfloat16 [8, 512, 1024], P('resp', 'seq'), may hold values from -5984 to 5984
- row_lse: bfloat16 [8, 512, 8], P('resp', 'seq'), as said below
- row_delta: bfloat16 [8, 512, 8], P('resp', 'seq'), may hold values from -59904 to 59904
- prefix_keys: bfloat16 [65536, 128], P('seq'), may hold values from -6 to 6
- prefix_values: bfloat16 [65536, 128], P('seq'), may hold values from -6 to 6
- resp_len: int32 [8], P('resp'), may hold values from 128 to 512, as said below
- visible: int32 [8], P('resp'), may hold values from 32768 to 65536, as said below
Outputs:
- grad_queries: bfloat16 [8, 512, 1024], P('resp', 'seq')
- grad_keys: bfloat16 [65536, 128], P(('seq', 'resp'))
- grad_values: bfloat16 [65536, 128], P(('seq', 'resp'))
The draws below stay inside these ranges and needn't reach their ends.
Inputs may be any that keep to these rules, and one draw needn't show every extreme that they name: `row_lse`: each value lies between log(65536) - 0.05 and log(65536) + 3. `resp_len`: some response has exactly 512 live positions. `visible`: some response sees the whole prompt.
All inputs are finite; a program needn't handle non-finite values.
Results may differ from the reference program's by a relative error of at most 0.0059.
Values may be sent and summed in bfloat16 or wider, within the bound.
A program may use at most 64 MiB of HBM per device.

```python
import math
import jax
import jax.numpy as jnp
from jax import lax

HD = 128
HEADS = 8
PD = 2048
RESP_LEN = 512
PREFIX = 65536
RESPONSES = 8


def draw_row_lse(key, part):
    key = jax.random.fold_in(key, 11)
    spread = jax.random.uniform(key, (RESPONSES, RESP_LEN, HEADS), jnp.float32, 0.5, 2.5)
    return (math.log(PREFIX) + spread).astype(jnp.bfloat16)


def draw_resp_len(key, part):
    key = jax.random.fold_in(key, 23)
    first_key, second_key = jax.random.split(key)
    lengths = jax.random.randint(first_key, (RESPONSES,), RESP_LEN // 4, RESP_LEN + 1, jnp.int32)
    longest = jax.random.randint(second_key, (), 0, RESPONSES, jnp.int32)
    return lengths.at[longest].set(RESP_LEN)


def draw_visible(key, part):
    key = jax.random.fold_in(key, 37)
    first_key, second_key = jax.random.split(key)
    spans = jax.random.randint(first_key, (RESPONSES,), PREFIX // 2, PREFIX + 1, jnp.int32)
    widest = jax.random.randint(second_key, (), 0, RESPONSES, jnp.int32)
    return spans.at[widest].set(PREFIX)


def shard_levels(own_key, dims, shards, smallest, largest):
    def one(dim, blocks):
        draws = jax.random.uniform(jax.random.fold_in(jax.random.fold_in(own_key, 6), dim), (blocks,), jnp.float32, smallest / len(shards), largest / len(shards))
        return jnp.repeat(jnp.exp(draws), dims[dim] // blocks).reshape((-1,) + (1,) * (len(dims) - dim - 1))

    loudness = one(*shards[0])
    for cut in shards[1:]:
        loudness = loudness * one(*cut)
    return loudness


def centred(key, dims, deviation, limit, pieces=(), held_as=jnp.bfloat16):
    loudness = shard_levels(key, dims, pieces, -0.22, 0.18) if pieces else 1.0
    values = jax.random.normal(key, dims, jnp.float32) * deviation * loudness
    return jnp.minimum(jnp.maximum(values, -limit), limit).astype(held_as)


def setup_inputs(seed: int = 0) -> dict:
    seeds = jax.random.split(jax.random.key(seed), 9)
    return {
        "queries": centred(seeds[0], (RESPONSES, RESP_LEN, HEADS * HD), 1.0, 6.0, ((0, 8), (1, 32))),
        "grad_out": centred(seeds[1], (RESPONSES, RESP_LEN, HEADS * HD), 1000.0, 5984.0, ((0, 8), (1, 32))),
        "row_lse": draw_row_lse(jax.random.fold_in(seeds[8], 71), 0),
        "row_delta": centred(seeds[3], (RESPONSES, RESP_LEN, HEADS), 10000.0, 59904.0, ((0, 8), (1, 32))),
        "prefix_keys": centred(seeds[4], (PREFIX, HD), 1.0, 6.0, ((0, 32),)),
        "prefix_values": centred(seeds[5], (PREFIX, HD), 1.0, 6.0, ((0, 32),)),
        "resp_len": draw_resp_len(jax.random.fold_in(seeds[8], 71), 0),
        "visible": draw_visible(jax.random.fold_in(seeds[8], 71), 0),
    }


def reference(queries, grad_out, row_lse, row_delta, prefix_keys, prefix_values, resp_len, visible):
    score_scale = HD ** -0.5
    block_count = PREFIX // PD
    key_blocks = prefix_keys.astype(jnp.float32).reshape(block_count, PD, HD)
    value_blocks = prefix_values.astype(jnp.float32).reshape(block_count, PD, HD)
    position_blocks = jnp.arange(PREFIX, dtype=jnp.int32).reshape(block_count, PD)

    def per_response(carry, item):
        q_rows, do_rows, lse_rows, delta_rows, length, seen = item
        q_three = q_rows.astype(jnp.float32).reshape(RESP_LEN, HEADS, HD)
        do_three = do_rows.astype(jnp.float32).reshape(RESP_LEN, HEADS, HD)
        row_ok = jnp.arange(RESP_LEN, dtype=jnp.int32) < length
        lse_t = lse_rows.astype(jnp.float32).T[:, :, None]
        delta_t = delta_rows.astype(jnp.float32).T[:, :, None]

        def per_block(grad_q, block):
            key_rows, value_rows, positions = block
            scores = jnp.einsum("rhd,kd->hrk", q_three, key_rows) * score_scale
            allowed = row_ok[None, :, None] & (positions < seen)[None, None, :]
            probs = jnp.where(allowed, jnp.exp(scores - lse_t), 0.0)
            probs_b = lax.optimization_barrier(probs.astype(jnp.bfloat16)).astype(jnp.float32)
            grad_v = jnp.einsum("hrk,rhd->kd", probs_b, do_three)
            grad_probs = jnp.einsum("rhd,kd->hrk", do_three, value_rows)
            grad_scores = lax.optimization_barrier((probs * (grad_probs - delta_t)).astype(jnp.bfloat16)).astype(jnp.float32)
            grad_k = jnp.einsum("hrk,rhd->kd", grad_scores, q_three)
            grad_q = grad_q + jnp.einsum("hrk,kd->rhd", grad_scores, key_rows)
            return grad_q, (grad_k, grad_v)

        grad_q, (grad_ks, grad_vs) = lax.scan(per_block, jnp.zeros((RESP_LEN, HEADS, HD), jnp.float32), (key_blocks, value_blocks, position_blocks))
        carry = (carry[0] + grad_ks.reshape(PREFIX, HD), carry[1] + grad_vs.reshape(PREFIX, HD))
        return carry, (grad_q * score_scale).reshape(RESP_LEN, HEADS * HD).astype(jnp.bfloat16)

    zeros = jnp.zeros((PREFIX, HD), jnp.float32)
    (grad_keys, grad_values), grad_queries = lax.scan(per_response, (zeros, zeros), (queries, grad_out, row_lse, row_delta, resp_len, visible))
    return grad_queries, (grad_keys * score_scale).astype(jnp.bfloat16), grad_values.astype(jnp.bfloat16)
```

```python
import jax
import jax.numpy as jnp
from jax import lax
from jax.experimental import pallas as pl
from jax.experimental.pallas import tpu as pltpu
from jax.sharding import PartitionSpec as P

HD = 128
HEADS = 8
ROWS = 16
KEYS = 2048
TILE = 512
SLOT = ROWS * HEADS
LOG2E = 1.4426950408889634
SCALE = HD ** -0.5
MESH = pl.DeviceIdType.MESH
f32, bf16 = jnp.float32, jnp.bfloat16

PHASE_A = (((0, 0),), ((0, 1), (0, 3)), ((1, 0), (3, 0), (0, 2)), ((1, 1), (1, 3), (3, 1), (3, 3)))
PHASE_B = (((2, 1), (2, 3), (1, 2), (3, 2)), ((2, 0), (2, 2)))
KEY_ORDER = (2, 1, 3, 0)


def dot(a, b, ca, cb):
    return lax.dot_general(a, b, (((ca,), (cb,)), ((), ())), preferred_element_type=f32)


def kernel(q_in, do_in, lse_in, delta_in, k_in, v_in, len_in, vis_in, oq, ok, ov,
           gq, gd, km, kt, vm, dk, dv, dq, sq, rq, ps, pr, zs, zr,
           s_gather, r_z, r_gq, r_gd, s_dq, r_dq, s_pair, r_pair, s_zs, r_zs):
    seq, resp = lax.axis_index("seq"), lax.axis_index("resp")
    y, x, zl = seq // 8, (seq // 2) % 4, seq % 2
    zh, core = resp // 2, resp % 2

    def seq_peer(dy, dx, dz):
        return ((((y + dy) % 4) * 4 + (x + dx) % 4) * 2 + (zl + dz) % 2, resp)

    def resp_peer(dz, dc):
        return (seq, ((zh + dz) % 4) * 2 + (core + dc) % 2)

    barrier = pltpu.get_barrier_semaphore()
    peers = [seq_peer(dy, dx, dz) for dy in range(4) for dx in range(4) for dz in range(2) if (dy, dx, dz) != (0, 0, 0)]
    peers += [resp_peer(0, 1), resp_peer(1, 0), resp_peer(2, 0), resp_peer(3, 0)]
    for peer in peers:
        pl.semaphore_signal(barrier, inc=1, device_id=peer, device_id_type=MESH)

    live = seq * ROWS + lax.broadcasted_iota(jnp.int32, (ROWS, HD), 0) < len_in[0]
    for h in range(HEADS):
        cols = slice(h * HD, (h + 1) * HD)
        rows = slice(h * ROWS, (h + 1) * ROWS)
        gq[0, rows, :] = jnp.where(live, q_in[:, cols].astype(f32), 0.0).astype(bf16)
        gd[0, rows, :] = jnp.where(live, do_in[:, cols].astype(f32), 0.0).astype(bf16)
    lane = lax.broadcasted_iota(jnp.int32, (ROWS, SLOT), 1)
    spread = jnp.where(lane % ROWS == lax.broadcasted_iota(jnp.int32, (ROWS, SLOT), 0), 1.0, 0.0).astype(bf16)
    head_lane = lax.broadcasted_iota(jnp.int32, (HEADS, SLOT), 1)
    own_head = head_lane // ROWS == lax.broadcasted_iota(jnp.int32, (HEADS, SLOT), 0)
    live_lane = seq * ROWS + head_lane % ROWS < len_in[0]
    lse_row = jnp.sum(jnp.where(own_head, dot(lse_in[...], spread, 1, 0), 0.0), axis=0, keepdims=True)
    delta_row = jnp.sum(jnp.where(own_head & live_lane, dot(delta_in[...], spread, 1, 0), 0.0), axis=0, keepdims=True)
    which = lax.broadcasted_iota(jnp.int32, (ROWS, SLOT), 0)
    gq[0, SLOT:SLOT + ROWS, :] = jnp.where(which == 0, lse_row, jnp.where(which == 1, delta_row, 0.0)).astype(bf16)

    pl.semaphore_wait(barrier, len(peers))

    started = []

    def send(src, dst, send_sem, recv_sem, peer):
        copy = pltpu.make_async_remote_copy(
            src_ref=src, dst_ref=dst, send_sem=send_sem, recv_sem=recv_sem, device_id=peer, device_id_type=MESH)
        copy.start()
        started.append(copy)

    def arrived(dst, recv_sem):
        pltpu.make_async_remote_copy(
            src_ref=dst, dst_ref=dst, send_sem=s_gather.at[0], recv_sem=recv_sem,
            device_id=seq_peer(0, 0, 1), device_id_type=MESH).wait_recv()

    def pair(ref, dy, dx):
        return ref.at[pl.ds(2 * (dy * 4 + dx), 2)]

    count = [0]

    def gather_sem():
        count[0] += 1
        return s_gather.at[count[0] - 1]

    send(gq.at[0], gq.at[1], gather_sem(), r_z.at[0], seq_peer(0, 0, 1))
    send(gd.at[0], gd.at[1], gather_sem(), r_z.at[1], seq_peer(0, 0, 1))
    arrived(gq.at[1], r_z.at[0])
    arrived(gd.at[1], r_z.at[1])
    for step in (1, 3, 2):
        back = (4 - step) % 4
        send(pair(gq, 0, 0), pair(gq, 0, back), gather_sem(), r_gq.at[back], seq_peer(0, step, 0))
        send(pair(gd, 0, 0), pair(gd, back, 0), gather_sem(), r_gd.at[back * 4], seq_peer(step, 0, 0))
        send(pair(gd, 0, 0), pair(gd, 0, back), gather_sem(), r_gd.at[back], seq_peer(0, step, 0))
        send(pair(gq, 0, 0), pair(gq, back, 0), gather_sem(), r_gq.at[back * 4], seq_peer(step, 0, 0))

    def pass_on(step):
        arrived(pair(gq, 0, step), r_gq.at[step])
        for dy in (1, 3, 2):
            back = (4 - dy) % 4
            send(pair(gq, 0, step), pair(gq, back, step), gather_sem(), r_gq.at[back * 4 + step], seq_peer(dy, 0, 0))
        arrived(pair(gd, step, 0), r_gd.at[step * 4])
        for dx in (1, 3, 2):
            back = (4 - dx) % 4
            send(pair(gd, step, 0), pair(gd, step, back), gather_sem(), r_gd.at[step * 4 + back], seq_peer(0, dx, 0))

    def need(pairs):
        for dy, dx in pairs:
            if (dy, dx) == (0, 0):
                continue
            if dy:
                arrived(pair(gq, dy, dx), r_gq.at[dy * 4 + dx])
            if dx:
                arrived(pair(gd, dy, dx), r_gd.at[dy * 4 + dx])

    half = TILE // 2

    def block_start(dz, dc):
        return pl.multiple_of((((zh + dz) % 4) * 2 + (core + dc) % 2) * half, half)

    def seen_rows(dz, dc):
        first = seq * KEYS + block_start(dz, dc)
        return first + lax.broadcasted_iota(jnp.int32, (half, HD), 0) < vis_in[0]

    for dz in range(4):
        for dc in range(2):
            src = pl.ds(block_start(dz, dc), half)
            dst = slice((dz * 2 + dc) * half, (dz * 2 + dc + 1) * half)
            block = jnp.where(seen_rows(dz, dc), k_in[src, :].astype(f32), 0.0)
            km[dst, :] = block.astype(bf16)
            kt[:, dst] = block.T.astype(bf16)
            vm[dst, :] = v_in[src, :]

    def attend(pairs, at, k0, first_q, first_k):
        own = slice(at, at + 256 * len(pairs))
        qb = jnp.concatenate([gq[2 * (a * 4 + b):2 * (a * 4 + b) + 2, 0:SLOT, :].reshape(256, HD) for a, b in pairs], axis=0)
        dob = jnp.concatenate([gd[2 * (a * 4 + b):2 * (a * 4 + b) + 2].reshape(256, HD) for a, b in pairs], axis=0)
        slots = [2 * (a * 4 + b) + c for a, b in pairs for c in range(2)]
        stats = [gq[s, SLOT:SLOT + ROWS, :].astype(f32) for s in slots]
        lse = jnp.concatenate([s[0:1, :] for s in stats], axis=1) * LOG2E
        delta = jnp.concatenate([s[1:2, :] for s in stats], axis=1)
        keys = pl.ds(k0, TILE)
        kb, vb = km[keys, :], vm[keys, :]
        probs = jnp.exp2(dot(kb, qb, 1, 1) * (SCALE * LOG2E) - lse)
        grads = (probs * (dot(vb, dob, 1, 1) - delta)).astype(bf16)
        probs = probs.astype(bf16)
        part_q = dot(kt[:, keys], grads, 1, 0)
        part_v = dot(probs, dob, 1, 0)
        part_k = dot(grads, qb, 1, 0)
        if first_q:
            dq[:, own] = part_q
        else:
            dq[:, own] += part_q
        if first_k:
            dk[keys, :] = part_k
            dv[keys, :] = part_v
        else:
            dk[keys, :] += part_k
            dv[keys, :] += part_v

    def send_queries(pairs, at):
        for n, (dy, dx) in enumerate(pairs):
            for dz in range(2):
                s = 2 * (dy * 4 + dx) + dz
                lanes = slice(at + (2 * n + dz) * SLOT, at + (2 * n + dz + 1) * SLOT)
                if s == 0:
                    rq[0] = dq[:, lanes].astype(bf16)
                else:
                    sq[s] = dq[:, lanes].astype(bf16)
                    send(sq.at[s], rq.at[s], s_dq.at[s], r_dq.at[s], seq_peer(dy, dx, dz))

    for n, pairs in enumerate(PHASE_A):
        need(pairs)
        width = 256 * len(pairs)
        dq[:, 0:width] = jnp.zeros((HD, width), f32)

        def one(i, carry, pairs=pairs, n=n):
            attend(pairs, 0, pl.multiple_of(i * TILE, TILE), False, n == 0)
            return carry

        lax.fori_loop(0, KEYS // TILE, one, 0)
        send_queries(pairs, 0)
        if n == 0:
            pass_on(1)
            pass_on(3)
        if n == 1:
            pass_on(2)

    def finish_keys(dz):
        for dc in (1, 0):
            rows = slice((dz * 2 + dc) * half, (dz * 2 + dc + 1) * half)
            seen = seen_rows(dz, dc)
            for n, total in enumerate((dk, dv)):
                part = jnp.where(seen, total[rows, :], 0.0)
                if dc:
                    ps[dz, n * half:(n + 1) * half, :] = part.astype(bf16)
                else:
                    total[rows, :] = part
            if dc:
                send(ps.at[dz], pr.at[dz], s_pair.at[dz], r_pair.at[dz], resp_peer(0, 1))

    def pass_keys(dz):
        arrived(pr.at[dz], r_pair.at[dz])
        rows = slice(dz * 2 * half, (dz * 2 + 1) * half)
        for n, total in enumerate((dk, dv)):
            zs[dz, n * half:(n + 1) * half, :] = (
                total[rows, :] + pr[dz, n * half:(n + 1) * half, :].astype(f32)).astype(bf16)
        send(zs.at[dz], zr.at[dz], s_zs.at[dz], r_zs.at[dz], resp_peer(dz, 0))

    for pairs in PHASE_B:
        need(pairs)
    offsets = [0]
    for pairs in PHASE_B:
        offsets.append(offsets[-1] + 256 * len(pairs))

    for i, dz in enumerate(KEY_ORDER):
        for n, pairs in enumerate(PHASE_B):
            attend(pairs, offsets[n], dz * TILE, i == 0, False)
            if i == 3:
                send_queries(pairs, offsets[n])
        finish_keys(dz)
        if i:
            pass_keys(KEY_ORDER[i - 1])

    arrived(pr.at[0], r_pair.at[0])
    totals = [dk[0:half, :] + pr[0, 0:half, :].astype(f32), dv[0:half, :] + pr[0, half:TILE, :].astype(f32)]
    for dz in (2, 1, 3):
        arrived(zr.at[dz], r_zs.at[dz])
        totals = [t + zr[dz, n * half:(n + 1) * half, :].astype(f32) for n, t in enumerate(totals)]
    ok[...] = (totals[0] * SCALE).astype(bf16)
    ov[...] = totals[1].astype(bf16)

    total = rq[0].astype(f32)
    for s in range(1, 32):
        arrived(rq.at[s], r_dq.at[s])
        total += rq[s].astype(f32)
    total = (total.T * SCALE).astype(bf16)
    for h in range(HEADS):
        oq[:, h * HD:(h + 1) * HD] = total[h * ROWS:(h + 1) * ROWS, :]
    for copy in started:
        copy.wait_send()


def on_device(queries, grad_out, row_lse, row_delta, prefix_keys, prefix_values, resp_len, visible):
    vmem, smem = pl.BlockSpec(memory_space=pltpu.VMEM), pl.BlockSpec(memory_space=pltpu.SMEM)
    dma = pltpu.SemaphoreType.DMA
    owned = KEYS // 8
    grad_queries, grad_keys, grad_values = pl.pallas_call(
        kernel,
        out_shape=(
            jax.ShapeDtypeStruct((ROWS, HEADS * HD), bf16),
            jax.ShapeDtypeStruct((owned, HD), bf16),
            jax.ShapeDtypeStruct((owned, HD), bf16),
        ),
        in_specs=[vmem] * 6 + [smem] * 2,
        out_specs=(vmem, vmem, vmem),
        scratch_shapes=[
            pltpu.VMEM((32, SLOT + ROWS, HD), bf16),
            pltpu.VMEM((32, SLOT, HD), bf16),
            pltpu.VMEM((KEYS, HD), bf16),
            pltpu.VMEM((HD, KEYS), bf16),
            pltpu.VMEM((KEYS, HD), bf16),
            pltpu.VMEM((KEYS, HD), f32),
            pltpu.VMEM((KEYS, HD), f32),
            pltpu.VMEM((HD, 2048), f32),
            pltpu.VMEM((32, HD, SLOT), bf16),
            pltpu.VMEM((32, HD, SLOT), bf16),
            pltpu.VMEM((4, TILE, HD), bf16),
            pltpu.VMEM((4, TILE, HD), bf16),
            pltpu.VMEM((4, TILE, HD), bf16),
            pltpu.VMEM((4, TILE, HD), bf16),
            dma((32,)), dma((2,)), dma((16,)), dma((16,)),
            dma((32,)), dma((32,)), dma((4,)), dma((4,)), dma((4,)), dma((4,)),
        ],
        compiler_params=pltpu.CompilerParams(
            collective_id=0, has_side_effects=True, vmem_limit_bytes=48 * 1024 * 1024),
    )(queries[0], grad_out[0], row_lse[0].T, row_delta[0].T, prefix_keys, prefix_values, resp_len, visible)
    return grad_queries[None], grad_keys, grad_values


def solution(mesh):
    in_specs = (
        P("resp", "seq", None),
        P("resp", "seq", None),
        P("resp", "seq", None),
        P("resp", "seq", None),
        P("seq", None),
        P("seq", None),
        P("resp"),
        P("resp"),
    )
    out_specs = (P("resp", "seq", None), P(("seq", "resp"), None), P(("seq", "resp"), None))
    return jax.shard_map(
        on_device, mesh=mesh, in_specs=in_specs, out_specs=out_specs, check_vma=False
    )
```

```python
import jax
import jax.numpy as jnp
from jax import lax
from jax.experimental import pallas as pl
from jax.experimental.pallas import tpu as pltpu
from jax.sharding import PartitionSpec as P

HD = 128
HEADS = 8
ROWS = 16
KEYS = 2048
TILE = 512
SLOT = ROWS * HEADS
DO = SLOT + ROWS
LOG2E = 1.4426950408889634
SCALE = HD ** -0.5
MESH = pl.DeviceIdType.MESH
f32, bf16 = jnp.float32, jnp.bfloat16

ALONG = (1, 3, 2)
FAR = tuple((dy, dx) for dy in ALONG for dx in ALONG)
OWN = ((0, 0, 0),)
NEAR_0 = ((0, 1, 0), (0, 3, 0), (1, 0, 0), (3, 0, 0))
TWO_0 = ((0, 2, 0), (2, 0, 0))
PARTNER = ((0, 0, 1),)
LINE_1 = tuple((dy, dx, 1) for dy, dx, _ in NEAR_0 + TWO_0)
FAR_0 = tuple((dy, dx, 0) for dy, dx in FAR)
FAR_1 = tuple((dy, dx, 1) for dy, dx in FAR)
ORDER = OWN + NEAR_0 + TWO_0 + PARTNER + LINE_1 + FAR_0 + FAR_1
QUARTER = TILE // 4
PIECES = (
    ((2, 0, 0, 256), (2, 1, 0, 256)),
    ((1, 0, 0, 128), (3, 0, 0, 128), (1, 1, 0, 128), (3, 1, 0, 128)),
    ((1, 0, 128, 128), (3, 0, 128, 128), (1, 1, 128, 128), (3, 1, 128, 128)),
    ((0, 0, 0, 256), (0, 1, 0, 256)),
)


def dot(a, b, ca, cb):
    return lax.dot_general(a, b, (((ca,), (cb,)), ((), ())), preferred_element_type=f32)


def kernel(q_in, do_in, lse_in, delta_in, k_in, v_in, len_in, vis_in, oq, ok, ov,
           q_own, do_own, lse_own, delta_own, k_own, vm, rows_all, km, kt, dk, dv, dq, sq, r1, s2, r2, s3, r3,
           ps, pr, zs, zr, s_in, s_gather, r_slot, r_fq, r_fd, s_dq, r_dq, s_pair, r_pair, s_zs, r_zs):
    seq, resp = lax.axis_index("seq"), lax.axis_index("resp")
    y, x, zl = seq // 8, (seq // 2) % 4, seq % 2
    zh, core = resp // 2, resp % 2

    def seq_peer(dy, dx, dz):
        return ((((y + dy) % 4) * 4 + (x + dx) % 4) * 2 + (zl + dz) % 2, resp)

    def resp_peer(dz, dc):
        return (seq, ((zh + dz) % 4) * 2 + (core + dc) % 2)

    loads = [pltpu.make_async_copy(src, dst, s_in.at[n]) for n, (src, dst) in enumerate(
        ((q_in, q_own), (do_in, do_own), (lse_in, lse_own), (delta_in, delta_own), (k_in, k_own)))]
    for load in loads:
        load.start()

    barrier = pltpu.get_barrier_semaphore()
    peers = [seq_peer(0, 0, 1)] + [seq_peer(d, 0, 0) for d in (1, 2, 3)] + [seq_peer(0, d, 0) for d in (1, 2, 3)]
    peers += [resp_peer(0, 1), resp_peer(1, 0), resp_peer(2, 0), resp_peer(3, 0)]
    for peer in peers:
        pl.semaphore_signal(barrier, inc=1, device_id=peer, device_id_type=MESH)

    half = TILE // 2
    pieces = []
    for n, step in enumerate(PIECES):
        at = n * TILE
        for dz, dc, first, count in step:
            start = pl.multiple_of((((zh + dz) % 4) * 2 + (core + dc) % 2) * half + first, QUARTER)
            pieces.append((n, start, slice(at, at + count), count))
            at += count
    for n, start, rows, count in pieces:
        loads.append(pltpu.make_async_copy(v_in.at[pl.ds(start, count)], vm.at[rows], s_in.at[len(loads)]))
        loads[-1].start()

    for load in loads[:4]:
        load.wait()
    live = seq * ROWS + lax.broadcasted_iota(jnp.int32, (ROWS, HD), 0) < len_in[0]
    for h in range(HEADS):
        cols = slice(h * HD, (h + 1) * HD)
        rows_all[0, h * ROWS:(h + 1) * ROWS, :] = jnp.where(live, q_own[:, cols].astype(f32), 0.0).astype(bf16)
        rows_all[0, DO + h * ROWS:DO + (h + 1) * ROWS, :] = jnp.where(live, do_own[:, cols].astype(f32), 0.0).astype(bf16)
    lane = lax.broadcasted_iota(jnp.int32, (ROWS, SLOT), 1)
    spread = jnp.where(lane % ROWS == lax.broadcasted_iota(jnp.int32, (ROWS, SLOT), 0), 1.0, 0.0).astype(bf16)
    head_lane = lax.broadcasted_iota(jnp.int32, (HEADS, SLOT), 1)
    own_head = head_lane // ROWS == lax.broadcasted_iota(jnp.int32, (HEADS, SLOT), 0)
    live_lane = seq * ROWS + head_lane % ROWS < len_in[0]
    lse_row = jnp.sum(jnp.where(own_head, dot(lse_own[...], spread, 1, 0), 0.0), axis=0, keepdims=True)
    delta_row = jnp.sum(jnp.where(own_head & live_lane, dot(delta_own[...], spread, 1, 0), 0.0), axis=0, keepdims=True)
    which = lax.broadcasted_iota(jnp.int32, (ROWS, SLOT), 0)
    rows_all[0, SLOT:DO, :] = jnp.where(which == 0, lse_row, jnp.where(which == 1, delta_row, 0.0)).astype(bf16)

    pl.semaphore_wait(barrier, len(peers))

    started = []

    def send(src, dst, send_sem, recv_sem, peer):
        copy = pltpu.make_async_remote_copy(
            src_ref=src, dst_ref=dst, send_sem=send_sem, recv_sem=recv_sem, device_id=peer, device_id_type=MESH)
        copy.start()
        started.append(copy)

    waited = set()

    def arrived(dst, recv_sem, name):
        if name in waited:
            return
        waited.add(name)
        pltpu.make_async_remote_copy(
            src_ref=dst, dst_ref=dst, send_sem=s_gather.at[0], recv_sem=recv_sem,
            device_id=seq_peer(0, 0, 1), device_id_type=MESH).wait_recv()

    sends = [0]

    def gather_sem():
        sends[0] += 1
        return s_gather.at[sends[0] - 1]

    def place(dy, dx):
        return (dy % 4) * 4 + dx % 4

    def slot(dy, dx, dz):
        return 2 * place(dy, dx) + dz

    def q_part(n):
        return rows_all.at[n, 0:DO]

    def do_part(n):
        return rows_all.at[n, DO:DO + SLOT]

    def along_lines(dz):
        for step in ALONG:
            for dy, dx in ((0, step), (step, 0)):
                at = slot(-dy, -dx, dz)
                send(rows_all.at[dz], rows_all.at[at], gather_sem(), r_slot.at[at], seq_peer(dy, dx, 0))

    def get(slots):
        for dy, dx, dz in slots:
            at = slot(dy, dx, dz)
            if dy and dx:
                arrived(q_part(at), r_fq.at[at], (at, "q"))
                arrived(do_part(at), r_fd.at[at], (at, "do"))
            elif at:
                arrived(rows_all.at[at], r_slot.at[at], at)

    def pass_on(slots):
        get(slots)
        for step in ALONG:
            for dy, dx, dz in slots:
                at = slot(dy, dx, dz)
                if dx:
                    to = slot(-step, dx, dz)
                    send(q_part(at), q_part(to), gather_sem(), r_fq.at[to], seq_peer(step, 0, 0))
                else:
                    to = slot(dy, -step, dz)
                    send(do_part(at), do_part(to), gather_sem(), r_fd.at[to], seq_peer(0, step, 0))

    send(rows_all.at[0], rows_all.at[1], gather_sem(), r_slot.at[1], seq_peer(0, 0, 1))
    along_lines(0)

    def seen_rows(start, count):
        return seq * KEYS + start + lax.broadcasted_iota(jnp.int32, (count, HD), 0) < vis_in[0]

    loads[4].wait()
    for n, start, rows, count in pieces:
        block = jnp.where(seen_rows(start, count), k_own[pl.ds(start, count), :].astype(f32), 0.0)
        km[rows, :] = block.astype(bf16)
        kt[:, rows] = block.T.astype(bf16)
    for load in loads[5:]:
        load.wait()

    def lanes(slots):
        at = ORDER.index(slots[0])
        return slice(at * SLOT, (at + len(slots)) * SLOT)

    def attend(slots, k0, tile, first_q, first_k):
        own = lanes(slots)
        places = [slot(*name) for name in slots]
        qb = jnp.concatenate([rows_all[p, 0:SLOT, :] for p in places], axis=0)
        dob = jnp.concatenate([rows_all[p, DO:DO + SLOT, :] for p in places], axis=0)
        stats = [rows_all[p, SLOT:DO, :].astype(f32) for p in places]
        lse = jnp.concatenate([s[0:1, :] for s in stats], axis=1) * LOG2E
        delta = jnp.concatenate([s[1:2, :] for s in stats], axis=1)
        keys = pl.ds(k0, tile)
        kb, vb = km[keys, :], vm[keys, :]
        probs = jnp.exp2(dot(kb, qb, 1, 1) * (SCALE * LOG2E) - lse)
        grads = (probs * (dot(vb, dob, 1, 1) - delta)).astype(bf16)
        probs = probs.astype(bf16)
        part_q = dot(kt[:, keys], grads, 1, 0)
        part_v = dot(probs, dob, 1, 0)
        part_k = dot(grads, qb, 1, 0)
        if first_q:
            dq[:, own] = part_q
        else:
            dq[:, own] += part_q
        if first_k:
            dk[keys, :] = part_k
            dv[keys, :] = part_v
        else:
            dk[keys, :] += part_k
            dv[keys, :] += part_v

    def source(c, n, step):
        return (c * 4 + n) * 3 + step - 1

    def send_queries(slots):
        for dy, dx, dz in slots:
            step, other = (dy, dx) if dz else (dx, dy)
            if step == 0:
                continue
            n = slot(dy, dx, dz)
            to = source(dz, other, 4 - step)
            sq[n] = dq[:, lanes(((dy, dx, dz),))].astype(bf16)
            send(sq.at[n], r1.at[to], s_dq.at[n], r_dq.at[to], seq_peer(dy, 0, 0) if dz else seq_peer(0, dx, 0))

    def line_sum(c, n):
        total = dq[:, lanes((((0, n, 1) if c else (n, 0, 0)),))]
        for step in (1, 3, 2):
            at = source(c, n, step)
            arrived(r1.at[at], r_dq.at[at], ("r1", at))
            total += r1[at].astype(f32)
        return total

    def send_line(c, n):
        at = c * 3 + n - 1
        to = c * 3 + (4 - n) - 1
        s2[at] = line_sum(c, n).astype(bf16)
        send(s2.at[at], r2.at[to], s_dq.at[32 + at], r_dq.at[24 + to], seq_peer(n, 0, 0) if c == 0 else seq_peer(0, n, 0))

    def own_sum(c):
        total = line_sum(c, 0)
        for n in (1, 2, 3):
            at = c * 3 + n - 1
            arrived(r2.at[at], r_dq.at[24 + at], ("r2", at))
            total += r2[at].astype(f32)
        return total

    def finish_keys(n):
        for m, start, rows, count in pieces:
            if m != n:
                continue
            seen = seen_rows(start, count)
            for which, total in enumerate((dk, dv)):
                part = jnp.where(seen, total[rows, :], 0.0)
                at = rows.start - n * TILE - half
                if at < 0:
                    total[rows, :] = part
                else:
                    ps[n, which * half + at:which * half + at + count, :] = part.astype(bf16)
        send(ps.at[n], pr.at[n], s_pair.at[n], r_pair.at[n], resp_peer(0, 1))

    def pair_sums(n):
        arrived(pr.at[n], r_pair.at[n], ("pair", n))
        return [total[n * TILE:n * TILE + half, :] + pr[n, which * half:(which + 1) * half, :].astype(f32)
                for which, total in enumerate((dk, dv))]

    def pass_keys(n):
        sums = pair_sums(n)
        for m, (dz, _, _, count) in enumerate(PIECES[n][:len(PIECES[n]) // 2]):
            at = 0 if n == 0 else TILE * n + m * half
            for which in range(2):
                zs[at + which * count:at + (which + 1) * count, :] = sums[which][m * count:(m + 1) * count, :].astype(bf16)
            whole, sem = pl.ds(at, 2 * count), 2 * n + m
            send(zs.at[whole], zr.at[whole], s_zs.at[sem], r_zs.at[sem], resp_peer(dz, 0))

    def from_others(first, count):
        n = 1 + first // QUARTER
        sums = [part[first:first + count, :] for part in own_keys]
        for at, size, skip, sem in ((0, half, first, 0), (TILE * n, count, 0, 2 * n), (TILE * n + half, count, 0, 2 * n + 1)):
            arrived(zr.at[pl.ds(at, 2 * size)], r_zs.at[sem], ("zr", at))
            sums = [t + zr[at + which * size + skip:at + which * size + skip + count, :].astype(f32) for which, t in enumerate(sums)]
        ok[first:first + count, :] = (sums[0] * SCALE).astype(bf16)
        ov[first:first + count, :] = sums[1].astype(bf16)

    for n in range(2):
        attend(OWN, n * 1024, 1024, n == 0, True)
    get(PARTNER)
    along_lines(1)
    pass_on(NEAR_0)
    attend(NEAR_0, 0, 1024, True, False)
    pass_on(TWO_0)
    attend(NEAR_0, 1024, TILE, False, False)
    attend(TWO_0 + PARTNER, 0, 1024, True, False)
    pass_on(LINE_1[:4])
    attend(TWO_0 + PARTNER, 1024, TILE, False, False)
    pass_on(LINE_1[4:])
    for n in range(3):
        attend(LINE_1, n * TILE, TILE, n == 0, False)
    get(FAR_0)
    for n in range(3):
        attend(FAR_0, n * TILE, TILE, n == 0, False)
    get(FAR_1)
    for n in range(3):
        attend(FAR_1, n * TILE, TILE, n == 0, False)
        if n:
            pass_keys(n - 1)
        finish_keys(n)
    attend(FAR_1, 3 * TILE, TILE, False, False)
    pass_keys(2)
    send_queries(FAR_1)
    attend(FAR_0, 3 * TILE, TILE, False, False)
    send_queries(FAR_0)
    attend(PARTNER + LINE_1, 3 * TILE, TILE, False, False)
    send_queries(LINE_1)
    for n in (2, 1, 3):
        send_line(1, n)
    attend(NEAR_0 + TWO_0, 3 * TILE, TILE, False, False)
    send_queries(NEAR_0 + TWO_0)
    finish_keys(3)
    for n in (2, 1, 3):
        send_line(0, n)
    s3[...] = own_sum(1)
    send(s3, r3, s_dq.at[38], r_dq.at[30], seq_peer(0, 0, 1))
    own_keys = pair_sums(3)
    for n in range(2):
        from_others(n * QUARTER, QUARTER)
    total = own_sum(0)
    arrived(r3, r_dq.at[30], "r3")
    total = ((total + r3[...]).T * SCALE).astype(bf16)
    for h in range(HEADS):
        oq[:, h * HD:(h + 1) * HD] = total[h * ROWS:(h + 1) * ROWS, :]
    for copy in started:
        copy.wait_send()


def on_device(queries, grad_out, row_lse, row_delta, prefix_keys, prefix_values, resp_len, visible):
    vmem, smem, hbm = (pl.BlockSpec(memory_space=space) for space in (pltpu.VMEM, pltpu.SMEM, pltpu.HBM))
    dma = pltpu.SemaphoreType.DMA
    owned = KEYS // 8
    grad_queries, grad_keys, grad_values = pl.pallas_call(
        kernel,
        out_shape=(
            jax.ShapeDtypeStruct((ROWS, HEADS * HD), bf16),
            jax.ShapeDtypeStruct((owned, HD), bf16),
            jax.ShapeDtypeStruct((owned, HD), bf16),
        ),
        in_specs=[hbm] * 6 + [smem] * 2,
        out_specs=(vmem, vmem, vmem),
        scratch_shapes=[
            pltpu.VMEM((ROWS, HEADS * HD), bf16),
            pltpu.VMEM((ROWS, HEADS * HD), bf16),
            pltpu.VMEM((HEADS, ROWS), bf16),
            pltpu.VMEM((HEADS, ROWS), bf16),
            pltpu.VMEM((KEYS, HD), bf16),
            pltpu.VMEM((KEYS, HD), bf16),
            pltpu.VMEM((32, DO + SLOT, HD), bf16),
            pltpu.VMEM((KEYS, HD), bf16),
            pltpu.VMEM((HD, KEYS), bf16),
            pltpu.VMEM((KEYS, HD), f32),
            pltpu.VMEM((KEYS, HD), f32),
            pltpu.VMEM((HD, 32 * SLOT), f32),
            pltpu.VMEM((32, HD, SLOT), bf16),
            pltpu.VMEM((24, HD, SLOT), bf16),
            pltpu.VMEM((6, HD, SLOT), bf16),
            pltpu.VMEM((6, HD, SLOT), bf16),
            pltpu.VMEM((HD, SLOT), f32),
            pltpu.VMEM((HD, SLOT), f32),
            pltpu.VMEM((4, TILE, HD), bf16),
            pltpu.VMEM((4, TILE, HD), bf16),
            pltpu.VMEM((3 * TILE, HD), bf16),
            pltpu.VMEM((3 * TILE, HD), bf16),
            dma((17,)), dma((49,)), dma((32,)), dma((32,)), dma((32,)),
            dma((39,)), dma((31,)), dma((4,)), dma((4,)), dma((6,)), dma((6,)),
        ],
        compiler_params=pltpu.CompilerParams(
            collective_id=0, has_side_effects=True, vmem_limit_bytes=64 * 1024 * 1024),
    )(queries[0], grad_out[0], row_lse[0].T, row_delta[0].T, prefix_keys, prefix_values, resp_len, visible)
    return grad_queries[None], grad_keys, grad_values


def solution(mesh):
    in_specs = (
        P("resp", "seq", None),
        P("resp", "seq", None),
        P("resp", "seq", None),
        P("resp", "seq", None),
        P("seq", None),
        P("seq", None),
        P("resp"),
        P("resp"),
    )
    out_specs = (P("resp", "seq", None), P(("seq", "resp"), None), P(("seq", "resp"), None))
    return jax.shard_map(
        on_device, mesh=mesh, in_specs=in_specs, out_specs=out_specs, check_vma=False
    )
```

```python
import jax
import jax.numpy as jnp
from jax import lax
from jax.experimental import pallas as pl
from jax.experimental.pallas import tpu as pltpu
from jax.sharding import PartitionSpec as P

HD = 128
HEADS = 8
ROWS = 16
KEYS = 2048
TILE = 512
SLOT = ROWS * HEADS
DO = SLOT + ROWS
LOG2E = 1.4426950408889634
SCALE = HD ** -0.5
MESH = pl.DeviceIdType.MESH
f32, bf16 = jnp.float32, jnp.bfloat16

ALONG = (1, 3, 2)
FAR = tuple((dy, dx) for dy in ALONG for dx in ALONG)
OWN = ((0, 0, 0),)
NEAR_0 = ((0, 1, 0), (0, 3, 0), (1, 0, 0), (3, 0, 0))
TWO_0 = ((0, 2, 0), (2, 0, 0))
PARTNER = ((0, 0, 1),)
LINE_1 = tuple((dy, dx, 1) for dy, dx, _ in NEAR_0 + TWO_0)
FAR_0 = tuple((dy, dx, 0) for dy, dx in FAR)
FAR_1 = tuple((dy, dx, 1) for dy, dx in FAR)
ORDER = OWN + TWO_0 + NEAR_0 + PARTNER + LINE_1 + FAR_0 + FAR_1
QUARTER = TILE // 4
PIECES = (
    ((2, 0, 0, 256), (2, 1, 0, 256)),
    ((1, 0, 0, 128), (3, 0, 0, 128), (1, 1, 0, 128), (3, 1, 0, 128)),
    ((1, 0, 128, 128), (3, 0, 128, 128), (1, 1, 128, 128), (3, 1, 128, 128)),
    ((0, 0, 0, 256), (0, 1, 0, 256)),
)


def dot(a, b, ca, cb):
    return lax.dot_general(a, b, (((ca,), (cb,)), ((), ())), preferred_element_type=f32)


def kernel(q_in, do_in, lse_in, delta_in, k_in, v_in, len_in, vis_in, oq, ok, ov,
           q_own, do_own, lse_own, delta_own, k_own, vm, rows_all, km, kt, dk, dv, dq, sq, r1, s2, r2, s3, r3,
           ps, pr, zs, zr, s_in, s_gather, r_line, r_fq, r_fd, s_dq, r_dq, s_pair, r_pair, s_zs, r_zs, near_sem, far_sem):
    seq, resp = lax.axis_index("seq"), lax.axis_index("resp")
    y, x, zl = seq // 8, (seq // 2) % 4, seq % 2
    zh, core = resp // 2, resp % 2

    def seq_peer(dy, dx, dz):
        return ((((y + dy) % 4) * 4 + (x + dx) % 4) * 2 + (zl + dz) % 2, resp)

    def resp_peer(dz, dc):
        return (seq, ((zh + dz) % 4) * 2 + (core + dc) % 2)

    loads = [pltpu.make_async_copy(src, dst, s_in.at[n]) for n, (src, dst) in enumerate(
        ((q_in, q_own), (do_in, do_own), (lse_in, lse_own), (delta_in, delta_own), (k_in, k_own)))]
    for load in loads:
        load.start()

    barrier = pltpu.get_barrier_semaphore()
    z_side = (seq_peer(0, 0, 1)[0], ((zh + 2 * zl + 3) % 4) * 2 + core)
    neighbours = [seq_peer(0, 0, 1), z_side] + [seq_peer(dy, dx, 0) for dy, dx in ((0, 1), (0, 3), (1, 0), (3, 0))]
    for peer in neighbours + [resp_peer(0, 1)]:
        pl.semaphore_signal(barrier, inc=1, device_id=peer, device_id_type=MESH)

    half = TILE // 2
    pieces = []
    for n, step in enumerate(PIECES):
        at = n * TILE
        for dz, dc, first, count in step:
            start = pl.multiple_of((((zh + dz) % 4) * 2 + (core + dc) % 2) * half + first, QUARTER)
            pieces.append((n, start, slice(at, at + count), count))
            at += count
    for n, start, rows, count in pieces:
        loads.append(pltpu.make_async_copy(v_in.at[pl.ds(start, count)], vm.at[rows], s_in.at[len(loads)]))
        loads[-1].start()

    for load in loads[:4]:
        load.wait()
    live = seq * ROWS + lax.broadcasted_iota(jnp.int32, (ROWS, HD), 0) < len_in[0]
    for h in range(HEADS):
        cols = slice(h * HD, (h + 1) * HD)
        rows_all[0, 0, 0, h * ROWS:(h + 1) * ROWS, :] = jnp.where(live, q_own[:, cols].astype(f32), 0.0).astype(bf16)
        rows_all[0, 0, 0, DO + h * ROWS:DO + (h + 1) * ROWS, :] = jnp.where(live, do_own[:, cols].astype(f32), 0.0).astype(bf16)
    lane = lax.broadcasted_iota(jnp.int32, (ROWS, SLOT), 1)
    spread = jnp.where(lane % ROWS == lax.broadcasted_iota(jnp.int32, (ROWS, SLOT), 0), 1.0, 0.0).astype(bf16)
    head_lane = lax.broadcasted_iota(jnp.int32, (HEADS, SLOT), 1)
    own_head = head_lane // ROWS == lax.broadcasted_iota(jnp.int32, (HEADS, SLOT), 0)
    live_lane = seq * ROWS + head_lane % ROWS < len_in[0]
    lse_row = jnp.sum(jnp.where(own_head, dot(lse_own[...], spread, 1, 0), 0.0), axis=0, keepdims=True)
    delta_row = jnp.sum(jnp.where(own_head & live_lane, dot(delta_own[...], spread, 1, 0), 0.0), axis=0, keepdims=True)
    which = lax.broadcasted_iota(jnp.int32, (ROWS, SLOT), 0)
    rows_all[0, 0, 0, SLOT:DO, :] = jnp.where(which == 0, lse_row, jnp.where(which == 1, delta_row, 0.0)).astype(bf16)

    pl.semaphore_wait(barrier, len(neighbours) + 1)
    for peer in neighbours:
        pl.semaphore_signal(near_sem, inc=1, device_id=peer, device_id_type=MESH)

    started = []

    def send(src, dst, send_sem, recv_sem, peer):
        copy = pltpu.make_async_remote_copy(
            src_ref=src, dst_ref=dst, send_sem=send_sem, recv_sem=recv_sem, device_id=peer, device_id_type=MESH)
        copy.start()
        started.append(copy)

    waited = set()

    def arrived(dst, recv_sem, name):
        if name in waited:
            return
        waited.add(name)
        pltpu.make_async_remote_copy(
            src_ref=dst, dst_ref=dst, send_sem=s_gather.at[0], recv_sem=recv_sem,
            device_id=seq_peer(0, 0, 1), device_id_type=MESH).wait_recv()

    sends = [0]

    def gather_sem():
        sends[0] += 1
        return s_gather.at[sends[0] - 1]

    def rows_of(dy, dx, dz):
        return rows_all.at[dz, dy % 4, dx % 4]

    def along_lines(dz, steps=ALONG):
        for step in steps:
            for n, (dy, dx) in enumerate(((0, step), (step, 0))):
                send(rows_of(0, 0, dz), rows_of(-dy, -dx, dz), gather_sem(), r_line.at[dz * 6 + n * 3 + 3 - step], seq_peer(dy, dx, 0))

    def get(slots):
        for dy, dx, dz in slots:
            if not dy and not dx:
                arrived(rows_of(0, 0, 1), r_line.at[12], "z")
            elif not dy or not dx:
                sem = dz * 6 + (3 if dy else 0) + dy + dx - 1
                arrived(rows_of(dy, dx, dz), r_line.at[sem], ("line", sem))
            else:
                arrived(queries_from(dz, dy), r_fq.at[dz * 3 + dy - 1], ("q", dz, dy))
                arrived(grads_from(dz, dx), r_fd.at[dz * 3 + dx - 1], ("do", dz, dx))

    def queries_from(dz, dy):
        return rows_all.at[dz, dy % 4, 1:4, 0:DO]

    def grads_from(dz, dx):
        return rows_all.at[dz, 1:4, dx % 4, DO:DO + SLOT]

    def pass_on(dz):
        for step in ALONG:
            sem = dz * 3 + 3 - step
            send(queries_from(dz, 0), queries_from(dz, -step), gather_sem(), r_fq.at[sem], seq_peer(step, 0, 0))
            send(grads_from(dz, 0), grads_from(dz, -step), gather_sem(), r_fd.at[sem], seq_peer(0, step, 0))

    send(rows_of(0, 0, 0), rows_of(0, 0, 1), gather_sem(), r_line.at[12], seq_peer(0, 0, 1))
    along_lines(0, (1, 3))

    def meet_far():
        pl.semaphore_wait(near_sem, len(neighbours))
        for dz in (1, 3):
            pl.semaphore_signal(far_sem, inc=1, device_id=resp_peer(dz, 0), device_id_type=MESH)

    def seen_rows(start, count):
        return seq * KEYS + start + lax.broadcasted_iota(jnp.int32, (count, HD), 0) < vis_in[0]

    loads[4].wait()
    for n, start, rows, count in pieces:
        block = jnp.where(seen_rows(start, count), k_own[pl.ds(start, count), :].astype(f32), 0.0)
        km[rows, :] = block.astype(bf16)
        kt[:, rows] = block.T.astype(bf16)
    meet_far()
    along_lines(0, (2,))
    for load in loads[5:]:
        load.wait()

    def lanes(slots):
        at = ORDER.index(slots[0])
        return slice(at * SLOT, (at + len(slots)) * SLOT)

    def attend(slots, k0, tile, first_q, first_k):
        own = lanes(slots)
        qb = jnp.concatenate([rows_all[dz, dy, dx, 0:SLOT, :] for dy, dx, dz in slots], axis=0)
        dob = jnp.concatenate([rows_all[dz, dy, dx, DO:DO + SLOT, :] for dy, dx, dz in slots], axis=0)
        stats = [rows_all[dz, dy, dx, SLOT:DO, :].astype(f32) for dy, dx, dz in slots]
        lse = jnp.concatenate([s[0:1, :] for s in stats], axis=1) * LOG2E
        delta = jnp.concatenate([s[1:2, :] for s in stats], axis=1)
        keys = pl.ds(k0, tile)
        kb, vb = km[keys, :], vm[keys, :]
        probs = jnp.exp2(dot(kb, qb, 1, 1) * (SCALE * LOG2E) - lse)
        grads = (probs * (dot(vb, dob, 1, 1) - delta)).astype(bf16)
        probs = probs.astype(bf16)
        part_q = dot(kt[:, keys], grads, 1, 0)
        part_v = dot(probs, dob, 1, 0)
        part_k = dot(grads, qb, 1, 0)
        if first_q:
            dq[:, own] = part_q
        else:
            dq[:, own] += part_q
        if first_k:
            dk[keys, :] = part_k
            dv[keys, :] = part_v
        else:
            dk[keys, :] += part_k
            dv[keys, :] += part_v

    def send_queries(c, far):
        for step in ALONG:
            for other in ((1, 2, 3) if far else (0,)):
                name = (step, other, 1) if c else (other, step, 0)
                sq[c, step - 1, other] = dq[:, lanes((name,))].astype(bf16)
            rows = slice(1, 4) if far else 0
            sem, to = c * 6 + 3 * far + step - 1, c * 6 + 3 * far + 3 - step
            send(sq.at[c, step - 1, rows], r1.at[c, 3 - step, rows], s_dq.at[sem], r_dq.at[to], seq_peer(step, 0, 0) if c else seq_peer(0, step, 0))

    def line_sum(c, n):
        total = dq[:, lanes((((0, n, 1) if c else (n, 0, 0)),))]
        far = 1 if n else 0
        for step in ALONG:
            rows, sem = (slice(1, 4) if far else 0), c * 6 + 3 * far + step - 1
            arrived(r1.at[c, step - 1, rows], r_dq.at[sem], ("r1", sem))
            total += r1[c, step - 1, n].astype(f32)
        return total

    def send_line(c, n):
        at = c * 3 + n - 1
        to = c * 3 + (4 - n) - 1
        s2[at] = line_sum(c, n).astype(bf16)
        send(s2.at[at], r2.at[to], s_dq.at[12 + at], r_dq.at[12 + to], seq_peer(0, n, 0) if c else seq_peer(n, 0, 0))

    def own_sum(c):
        total = line_sum(c, 0)
        for n in (1, 2, 3):
            at = c * 3 + n - 1
            arrived(r2.at[at], r_dq.at[12 + at], ("r2", at))
            total += r2[at].astype(f32)
        return total

    def finish_keys(n):
        for m, start, rows, count in pieces:
            if m != n:
                continue
            seen = seen_rows(start, count)
            for which, total in enumerate((dk, dv)):
                part = jnp.where(seen, total[rows, :], 0.0)
                at = rows.start - n * TILE - half
                if at < 0:
                    total[rows, :] = part
                else:
                    ps[n, which * half + at:which * half + at + count, :] = part.astype(bf16)
        send(ps.at[n], pr.at[n], s_pair.at[n], r_pair.at[n], resp_peer(0, 1))

    def pair_sums(n):
        arrived(pr.at[n], r_pair.at[n], ("pair", n))
        return [total[n * TILE:n * TILE + half, :] + pr[n, which * half:(which + 1) * half, :].astype(f32)
                for which, total in enumerate((dk, dv))]

    def pass_farthest():
        sums = pair_sums(0)
        for which in range(2):
            for part in range(2):
                at = (part * 2 + which) * QUARTER
                zs[at:at + QUARTER, :] = sums[which][part * QUARTER:(part + 1) * QUARTER, :].astype(bf16)
        for at, count, sem, dz in ((half, QUARTER, 1, 1), (half + QUARTER, QUARTER, 6, 3), (0, half, 0, 2)):
            send(zs.at[pl.ds(at, count)], zr.at[pl.ds(at, count)], s_zs.at[sem], r_zs.at[sem], resp_peer(dz, 0))

    def pass_keys(n):
        sums = pair_sums(n)
        for m in range(2):
            at, sem = TILE * n + m * half, 2 * n + m
            for which in range(2):
                part = sums[which][m * QUARTER:(m + 1) * QUARTER, :]
                if n == 2 and m == which:
                    other = half + m * QUARTER
                    arrived(zr.at[pl.ds(other, QUARTER)], r_zs.at[1 + 5 * m], ("relay", m))
                    part += zr[other:other + QUARTER, :].astype(f32)
                zs[at + which * QUARTER:at + (which + 1) * QUARTER, :] = part.astype(bf16)
            send(zs.at[pl.ds(at, half)], zr.at[pl.ds(at, half)], s_zs.at[sem], r_zs.at[sem], resp_peer(1 + 2 * m, 0))

    def from_others(n):
        rows = slice((n - 1) * QUARTER, n * QUARTER)
        sums = [part[rows, :] for part in own_keys]
        for at, sem in ((TILE * n, 2 * n), (TILE * n + half, 2 * n + 1), (0, 0))[:4 - n]:
            arrived(zr.at[pl.ds(at, half)], r_zs.at[sem], ("zr", at))
            sums = [t + zr[at + which * QUARTER:at + (which + 1) * QUARTER, :].astype(f32) for which, t in enumerate(sums)]
        ok[rows, :] = (sums[0] * SCALE).astype(bf16)
        ov[rows, :] = sums[1].astype(bf16)

    for n in range(2):
        attend(OWN, n * 1024, 1024, n == 0, True)
    get(PARTNER)
    along_lines(1)
    get(NEAR_0)
    attend(NEAR_0 + PARTNER, 0, 1024, True, False)
    get(TWO_0)
    pass_on(0)
    attend(NEAR_0 + PARTNER, 1024, TILE, False, False)
    attend(TWO_0, 0, 1024, True, False)
    attend(TWO_0, 1024, TILE, False, False)
    get(LINE_1)
    pass_on(1)
    for n in range(3):
        attend(LINE_1, n * TILE, TILE, n == 0, False)
    get(FAR_0)
    for n in range(3):
        attend(FAR_0, n * TILE, TILE, n == 0, False)
    get(FAR_1)
    pl.semaphore_wait(far_sem, 2)
    for n in range(3):
        attend(FAR_1, n * TILE, TILE, n == 0, False)
        if n == 1:
            pass_farthest()
        if n == 2:
            pass_keys(1)
        finish_keys(n)
    attend(FAR_1, 3 * TILE, TILE, False, False)
    send_queries(1, 1)
    attend(FAR_0, 3 * TILE, TILE, False, False)
    pass_keys(2)
    send_queries(0, 1)
    attend(PARTNER + LINE_1, 3 * TILE, TILE, False, False)
    send_queries(1, 0)
    attend(TWO_0 + NEAR_0, 3 * TILE, TILE, False, False)
    send_queries(0, 0)
    finish_keys(3)
    for n in ALONG:
        send_line(1, n)
    for n in ALONG:
        send_line(0, n)
    s3[...] = own_sum(1)
    send(s3, r3, s_dq.at[18], r_dq.at[18], seq_peer(0, 0, 1))
    own_keys = pair_sums(3)
    for n in (1, 2):
        from_others(n)
    total = own_sum(0)
    arrived(r3, r_dq.at[18], "r3")
    total = ((total + r3[...]).T * SCALE).astype(bf16)
    for h in range(HEADS):
        oq[:, h * HD:(h + 1) * HD] = total[h * ROWS:(h + 1) * ROWS, :]
    for copy in started:
        copy.wait_send()


def on_device(queries, grad_out, row_lse, row_delta, prefix_keys, prefix_values, resp_len, visible):
    vmem, smem, hbm = (pl.BlockSpec(memory_space=space) for space in (pltpu.VMEM, pltpu.SMEM, pltpu.HBM))
    dma = pltpu.SemaphoreType.DMA
    owned = KEYS // 8
    grad_queries, grad_keys, grad_values = pl.pallas_call(
        kernel,
        out_shape=(
            jax.ShapeDtypeStruct((ROWS, HEADS * HD), bf16),
            jax.ShapeDtypeStruct((owned, HD), bf16),
            jax.ShapeDtypeStruct((owned, HD), bf16),
        ),
        in_specs=[hbm] * 6 + [smem] * 2,
        out_specs=(vmem, vmem, vmem),
        scratch_shapes=[
            pltpu.VMEM((ROWS, HEADS * HD), bf16),
            pltpu.VMEM((ROWS, HEADS * HD), bf16),
            pltpu.VMEM((HEADS, ROWS), bf16),
            pltpu.VMEM((HEADS, ROWS), bf16),
            pltpu.VMEM((KEYS, HD), bf16),
            pltpu.VMEM((KEYS, HD), bf16),
            pltpu.VMEM((2, 4, 4, DO + SLOT, HD), bf16),
            pltpu.VMEM((KEYS, HD), bf16),
            pltpu.VMEM((HD, KEYS), bf16),
            pltpu.VMEM((KEYS, HD), f32),
            pltpu.VMEM((KEYS, HD), f32),
            pltpu.VMEM((HD, 32 * SLOT), f32),
            pltpu.VMEM((2, 3, 4, HD, SLOT), bf16),
            pltpu.VMEM((2, 3, 4, HD, SLOT), bf16),
            pltpu.VMEM((6, HD, SLOT), bf16),
            pltpu.VMEM((6, HD, SLOT), bf16),
            pltpu.VMEM((HD, SLOT), f32),
            pltpu.VMEM((HD, SLOT), f32),
            pltpu.VMEM((4, TILE, HD), bf16),
            pltpu.VMEM((4, TILE, HD), bf16),
            pltpu.VMEM((3 * TILE, HD), bf16),
            pltpu.VMEM((3 * TILE, HD), bf16),
            dma((17,)), dma((25,)), dma((13,)), dma((6,)), dma((6,)),
            dma((19,)), dma((19,)), dma((4,)), dma((4,)), dma((7,)), dma((7,)),
            pltpu.SemaphoreType.REGULAR, pltpu.SemaphoreType.REGULAR,
        ],
        compiler_params=pltpu.CompilerParams(
            collective_id=0, has_side_effects=True, vmem_limit_bytes=64 * 1024 * 1024),
    )(queries[0], grad_out[0], row_lse[0].T, row_delta[0].T, prefix_keys, prefix_values, resp_len, visible)
    return grad_queries[None], grad_keys, grad_values


def solution(mesh):
    in_specs = (
        P("resp", "seq", None),
        P("resp", "seq", None),
        P("resp", "seq", None),
        P("resp", "seq", None),
        P("seq", None),
        P("seq", None),
        P("resp"),
        P("resp"),
    )
    out_specs = (P("resp", "seq", None), P(("seq", "resp"), None), P(("seq", "resp"), None))
    return jax.shard_map(
        on_device, mesh=mesh, in_specs=in_specs, out_specs=out_specs, check_vma=False
    )
```

```python
import jax
import jax.numpy as jnp
from jax import lax
from jax.experimental import pallas as pl
from jax.experimental.pallas import tpu as pltpu
from jax.sharding import PartitionSpec as P

HD = 128
HEADS = 8
ROWS = 16
KEYS = 2048
TILE = 512
SLOT = ROWS * HEADS
DO = SLOT + ROWS
LOG2E = 1.4426950408889634
SCALE = HD ** -0.5
MESH = pl.DeviceIdType.MESH
f32, bf16 = jnp.float32, jnp.bfloat16

ALONG = (1, 3, 2)
FAR = tuple((dy, dx) for dy in ALONG for dx in ALONG)
OWN = ((0, 0, 0),)
NEAR_0 = ((0, 1, 0), (0, 3, 0), (1, 0, 0), (3, 0, 0))
TWO_0 = ((0, 2, 0), (2, 0, 0))
PARTNER = ((0, 0, 1),)
LINE_1 = tuple((dy, dx, 1) for dy, dx, _ in NEAR_0 + TWO_0)
FAR_0 = tuple((dy, dx, 0) for dy, dx in FAR)
FAR_1 = tuple((dy, dx, 1) for dy, dx in FAR)
ORDER = OWN + TWO_0 + NEAR_0 + PARTNER + LINE_1 + FAR_0 + FAR_1
QUARTER = TILE // 4
PIECES = (
    ((2, 0, 0, 256), (2, 1, 0, 256)),
    ((1, 0, 0, 128), (3, 0, 0, 128), (1, 1, 0, 128), (3, 1, 0, 128)),
    ((1, 0, 128, 128), (3, 0, 128, 128), (1, 1, 128, 128), (3, 1, 128, 128)),
    ((0, 0, 0, 256), (0, 1, 0, 256)),
)


def dot(a, b, ca, cb):
    return lax.dot_general(a, b, (((ca,), (cb,)), ((), ())), preferred_element_type=f32)


def kernel(q_in, do_in, lse_in, delta_in, k_in, v_in, len_in, vis_in, oq, ok, ov,
           q_own, do_own, k_own, vm, rows_all, km, kt, dk, dv, dq, sq, r1, s2, r2, s3, r3,
           ps, pr, zs, zr, s_in, s_gather, r_line, r_fq, r_fd, s_dq, r_dq, s_pair, r_pair, s_zs, r_zs, near_sem, far_sem):
    seq, resp = lax.axis_index("seq"), lax.axis_index("resp")
    y, x, zl = seq // 8, (seq // 2) % 4, seq % 2
    zh, core = resp // 2, resp % 2

    def seq_peer(dy, dx, dz):
        return ((((y + dy) % 4) * 4 + (x + dx) % 4) * 2 + (zl + dz) % 2, resp)

    def resp_peer(dz, dc):
        return (seq, ((zh + dz) % 4) * 2 + (core + dc) % 2)

    loads = [pltpu.make_async_copy(src, dst, s_in.at[n]) for n, (src, dst) in enumerate(
        ((q_in, q_own), (do_in, do_own), (k_in, k_own)))]
    for load in loads:
        load.start()

    barrier = pltpu.get_barrier_semaphore()
    z_side = (seq_peer(0, 0, 1)[0], ((zh + 2 * zl + 3) % 4) * 2 + core)
    neighbours = [seq_peer(0, 0, 1), z_side] + [seq_peer(dy, dx, 0) for dy, dx in ((0, 1), (0, 3), (1, 0), (3, 0))]
    for peer in neighbours + [resp_peer(0, 1)]:
        pl.semaphore_signal(barrier, inc=1, device_id=peer, device_id_type=MESH)

    half = TILE // 2
    pieces = []
    for n, step in enumerate(PIECES):
        at = n * TILE
        for dz, dc, first, count in step:
            start = pl.multiple_of((((zh + dz) % 4) * 2 + (core + dc) % 2) * half + first, QUARTER)
            pieces.append((n, start, slice(at, at + count), count))
            at += count
    for n, start, rows, count in pieces:
        loads.append(pltpu.make_async_copy(v_in.at[pl.ds(start, count)], vm.at[rows], s_in.at[len(loads)]))
        loads[-1].start()

    for load in loads[:2]:
        load.wait()
    live = seq * ROWS + lax.broadcasted_iota(jnp.int32, (ROWS, HD), 0) < len_in[0]
    for h in range(HEADS):
        cols = slice(h * HD, (h + 1) * HD)
        rows_all[0, 0, 0, h * ROWS:(h + 1) * ROWS, :] = jnp.where(live, q_own[:, cols].astype(f32), 0.0).astype(bf16)
        rows_all[0, 0, 0, DO + h * ROWS:DO + (h + 1) * ROWS, :] = jnp.where(live, do_own[:, cols].astype(f32), 0.0).astype(bf16)
    lane = lax.broadcasted_iota(jnp.int32, (ROWS, SLOT), 1)
    spread = jnp.where(lane % ROWS == lax.broadcasted_iota(jnp.int32, (ROWS, SLOT), 0), 1.0, 0.0).astype(bf16)
    head_lane = lax.broadcasted_iota(jnp.int32, (HEADS, SLOT), 1)
    own_head = head_lane // ROWS == lax.broadcasted_iota(jnp.int32, (HEADS, SLOT), 0)
    live_lane = seq * ROWS + head_lane % ROWS < len_in[0]
    lse_row = jnp.sum(jnp.where(own_head, dot(lse_in[...], spread, 1, 0), 0.0), axis=0, keepdims=True)
    delta_row = jnp.sum(jnp.where(own_head & live_lane, dot(delta_in[...], spread, 1, 0), 0.0), axis=0, keepdims=True)
    which = lax.broadcasted_iota(jnp.int32, (ROWS, SLOT), 0)
    rows_all[0, 0, 0, SLOT:DO, :] = jnp.where(which == 0, lse_row, jnp.where(which == 1, delta_row, 0.0)).astype(bf16)

    pl.semaphore_wait(barrier, len(neighbours) + 1)
    for peer in neighbours:
        pl.semaphore_signal(near_sem, inc=1, device_id=peer, device_id_type=MESH)

    started = []

    def send(src, dst, send_sem, recv_sem, peer):
        copy = pltpu.make_async_remote_copy(
            src_ref=src, dst_ref=dst, send_sem=send_sem, recv_sem=recv_sem, device_id=peer, device_id_type=MESH)
        copy.start()
        started.append(copy)

    waited = set()

    def arrived(dst, recv_sem, name):
        if name in waited:
            return
        waited.add(name)
        pltpu.make_async_remote_copy(
            src_ref=dst, dst_ref=dst, send_sem=s_gather.at[0], recv_sem=recv_sem,
            device_id=seq_peer(0, 0, 1), device_id_type=MESH).wait_recv()

    sends = [0]

    def gather_sem():
        sends[0] += 1
        return s_gather.at[sends[0] - 1]

    def rows_of(dy, dx, dz):
        return rows_all.at[dz, dy % 4, dx % 4]

    def along_lines(dz, steps=ALONG):
        for step in steps:
            for n, (dy, dx) in enumerate(((0, step), (step, 0))):
                send(rows_of(0, 0, dz), rows_of(-dy, -dx, dz), gather_sem(), r_line.at[dz * 6 + n * 3 + 3 - step], seq_peer(dy, dx, 0))

    def get(slots):
        for dy, dx, dz in slots:
            if not dy and not dx:
                arrived(rows_of(0, 0, 1), r_line.at[12], "z")
            elif not dy or not dx:
                sem = dz * 6 + (3 if dy else 0) + dy + dx - 1
                arrived(rows_of(dy, dx, dz), r_line.at[sem], ("line", sem))
            else:
                arrived(queries_from(dz, dy), r_fq.at[dz * 3 + dy - 1], ("q", dz, dy))
                arrived(grads_from(dz, dx), r_fd.at[dz * 3 + dx - 1], ("do", dz, dx))

    def queries_from(dz, dy):
        return rows_all.at[dz, dy % 4, 1:4, 0:DO]

    def grads_from(dz, dx):
        return rows_all.at[dz, 1:4, dx % 4, DO:DO + SLOT]

    def pass_on(dz):
        for step in ALONG:
            sem = dz * 3 + 3 - step
            send(queries_from(dz, 0), queries_from(dz, -step), gather_sem(), r_fq.at[sem], seq_peer(step, 0, 0))
            send(grads_from(dz, 0), grads_from(dz, -step), gather_sem(), r_fd.at[sem], seq_peer(0, step, 0))

    send(rows_of(0, 0, 0), rows_of(0, 0, 1), gather_sem(), r_line.at[12], seq_peer(0, 0, 1))
    along_lines(0, (1, 3))

    def meet_far():
        pl.semaphore_wait(near_sem, len(neighbours))
        for dz in (1, 3):
            pl.semaphore_signal(far_sem, inc=1, device_id=resp_peer(dz, 0), device_id_type=MESH)

    def seen_rows(start, count):
        return seq * KEYS + start + lax.broadcasted_iota(jnp.int32, (count, HD), 0) < vis_in[0]

    loads[2].wait()
    for n, start, rows, count in pieces:
        block = jnp.where(seen_rows(start, count), k_own[pl.ds(start, count), :].astype(f32), 0.0)
        km[rows, :] = block.astype(bf16)
        kt[:, rows] = block.T.astype(bf16)
    meet_far()
    along_lines(0, (2,))
    for load in loads[3:]:
        load.wait()

    def lanes(slots):
        at = ORDER.index(slots[0])
        return slice(at * SLOT, (at + len(slots)) * SLOT)

    def attend(slots, k0, tile, first_q, first_k):
        own = lanes(slots)
        qb = jnp.concatenate([rows_all[dz, dy, dx, 0:SLOT, :] for dy, dx, dz in slots], axis=0)
        dob = jnp.concatenate([rows_all[dz, dy, dx, DO:DO + SLOT, :] for dy, dx, dz in slots], axis=0)
        stats = [rows_all[dz, dy, dx, SLOT:DO, :].astype(f32) for dy, dx, dz in slots]
        lse = jnp.concatenate([s[0:1, :] for s in stats], axis=1) * LOG2E
        delta = jnp.concatenate([s[1:2, :] for s in stats], axis=1)
        keys = pl.ds(k0, tile)
        kb, vb = km[keys, :], vm[keys, :]
        probs = jnp.exp2(dot(kb, qb, 1, 1) * (SCALE * LOG2E) - lse)
        grads = (probs * (dot(vb, dob, 1, 1) - delta)).astype(bf16)
        probs = probs.astype(bf16)
        part_q = dot(kt[:, keys], grads, 1, 0)
        part_v = dot(probs, dob, 1, 0)
        part_k = dot(grads, qb, 1, 0)
        if first_q:
            dq[:, own] = part_q
        else:
            dq[:, own] += part_q
        if first_k:
            dk[keys, :] = part_k
            dv[keys, :] = part_v
        else:
            dk[keys, :] += part_k
            dv[keys, :] += part_v

    def send_queries(c, far):
        for step in ALONG:
            for other in ((1, 2, 3) if far else (0,)):
                name = (step, other, 1) if c else (other, step, 0)
                sq[c, step - 1, other] = dq[:, lanes((name,))].astype(bf16)
            rows = slice(1, 4) if far else 0
            sem, to = c * 6 + 3 * far + step - 1, c * 6 + 3 * far + 3 - step
            send(sq.at[c, step - 1, rows], r1.at[c, 3 - step, rows], s_dq.at[sem], r_dq.at[to], seq_peer(step, 0, 0) if c else seq_peer(0, step, 0))

    def line_sum(c, n):
        total = dq[:, lanes((((0, n, 1) if c else (n, 0, 0)),))]
        far = 1 if n else 0
        for step in ALONG:
            rows, sem = (slice(1, 4) if far else 0), c * 6 + 3 * far + step - 1
            arrived(r1.at[c, step - 1, rows], r_dq.at[sem], ("r1", sem))
            total += r1[c, step - 1, n].astype(f32)
        return total

    def send_line(c, n):
        at = c * 3 + n - 1
        to = c * 3 + (4 - n) - 1
        s2[at] = line_sum(c, n).astype(bf16)
        send(s2.at[at], r2.at[to], s_dq.at[12 + at], r_dq.at[12 + to], seq_peer(0, n, 0) if c else seq_peer(n, 0, 0))

    def own_sum(c):
        total = line_sum(c, 0)
        for n in (1, 2, 3):
            at = c * 3 + n - 1
            arrived(r2.at[at], r_dq.at[12 + at], ("r2", at))
            total += r2[at].astype(f32)
        return total

    def finish_keys(n):
        for m, start, rows, count in pieces:
            if m != n:
                continue
            seen = seen_rows(start, count)
            for which, total in enumerate((dk, dv)):
                part = jnp.where(seen, total[rows, :], 0.0)
                at = rows.start - n * TILE - half
                if at < 0:
                    total[rows, :] = part
                else:
                    ps[n, which * half + at:which * half + at + count, :] = part.astype(bf16)
        send(ps.at[n], pr.at[n], s_pair.at[n], r_pair.at[n], resp_peer(0, 1))

    def pair_sums(n):
        arrived(pr.at[n], r_pair.at[n], ("pair", n))
        return [total[n * TILE:n * TILE + half, :] + pr[n, which * half:(which + 1) * half, :].astype(f32)
                for which, total in enumerate((dk, dv))]

    def pass_farthest():
        sums = pair_sums(0)
        for which in range(2):
            for part in range(2):
                at = (part * 2 + which) * QUARTER
                zs[at:at + QUARTER, :] = sums[which][part * QUARTER:(part + 1) * QUARTER, :].astype(bf16)
        for at, count, sem, dz in ((half, QUARTER, 1, 1), (half + QUARTER, QUARTER, 6, 3), (0, half, 0, 2)):
            send(zs.at[pl.ds(at, count)], zr.at[pl.ds(at, count)], s_zs.at[sem], r_zs.at[sem], resp_peer(dz, 0))

    def pass_keys(n):
        sums = pair_sums(n)
        for m in range(2):
            at, sem = TILE * n + m * half, 2 * n + m
            for which in range(2):
                part = sums[which][m * QUARTER:(m + 1) * QUARTER, :]
                if n == 2 and m == which:
                    other = half + m * QUARTER
                    arrived(zr.at[pl.ds(other, QUARTER)], r_zs.at[1 + 5 * m], ("relay", m))
                    part += zr[other:other + QUARTER, :].astype(f32)
                zs[at + which * QUARTER:at + (which + 1) * QUARTER, :] = part.astype(bf16)
            send(zs.at[pl.ds(at, half)], zr.at[pl.ds(at, half)], s_zs.at[sem], r_zs.at[sem], resp_peer(1 + 2 * m, 0))

    def from_others(n):
        rows = slice((n - 1) * QUARTER, n * QUARTER)
        sums = [part[rows, :] for part in own_keys]
        for at, sem in ((TILE * n, 2 * n), (TILE * n + half, 2 * n + 1), (0, 0))[:4 - n]:
            arrived(zr.at[pl.ds(at, half)], r_zs.at[sem], ("zr", at))
            sums = [t + zr[at + which * QUARTER:at + (which + 1) * QUARTER, :].astype(f32) for which, t in enumerate(sums)]
        ok[rows, :] = (sums[0] * SCALE).astype(bf16)
        ov[rows, :] = sums[1].astype(bf16)

    get(PARTNER)
    along_lines(1)
    for n in range(2):
        attend(OWN, n * 1024, 1024, n == 0, True)
    get(NEAR_0 + TWO_0)
    pass_on(0)
    attend(NEAR_0 + PARTNER, 0, 1024, True, False)
    attend(NEAR_0 + PARTNER, 1024, TILE, False, False)
    attend(TWO_0, 0, 1024, True, False)
    attend(TWO_0, 1024, TILE, False, False)
    get(LINE_1)
    pass_on(1)
    for n in range(3):
        attend(LINE_1, n * TILE, TILE, n == 0, False)
    get(FAR_0)
    for n in range(3):
        attend(FAR_0, n * TILE, TILE, n == 0, False)
    get(FAR_1)
    pl.semaphore_wait(far_sem, 2)
    for n in range(3):
        attend(FAR_1, n * TILE, TILE, n == 0, False)
        if n == 1:
            pass_farthest()
        if n == 2:
            pass_keys(1)
        finish_keys(n)
    attend(FAR_1, 3 * TILE, TILE, False, False)
    send_queries(1, 1)
    attend(FAR_0, 3 * TILE, TILE, False, False)
    pass_keys(2)
    send_queries(0, 1)
    attend(PARTNER + LINE_1, 3 * TILE, TILE, False, False)
    send_queries(1, 0)
    attend(TWO_0 + NEAR_0, 3 * TILE, TILE, False, False)
    send_queries(0, 0)
    finish_keys(3)
    for n in ALONG:
        send_line(1, n)
    for n in ALONG:
        send_line(0, n)
    s3[...] = own_sum(1).astype(bf16)
    send(s3, r3, s_dq.at[18], r_dq.at[18], seq_peer(0, 0, 1))
    own_keys = pair_sums(3)
    for n in (1, 2):
        from_others(n)
    total = own_sum(0)
    arrived(r3, r_dq.at[18], "r3")
    total = ((total + r3[...].astype(f32)).T * SCALE).astype(bf16)
    for h in range(HEADS):
        oq[0, :, h * HD:(h + 1) * HD] = total[h * ROWS:(h + 1) * ROWS, :]
    for copy in started:
        copy.wait_send()


def on_device(queries, grad_out, row_lse, row_delta, prefix_keys, prefix_values, resp_len, visible):
    vmem, smem, hbm = (pl.BlockSpec(memory_space=space) for space in (pltpu.VMEM, pltpu.SMEM, pltpu.HBM))
    dma = pltpu.SemaphoreType.DMA
    owned = KEYS // 8
    return pl.pallas_call(
        kernel,
        out_shape=(
            jax.ShapeDtypeStruct((1, ROWS, HEADS * HD), bf16),
            jax.ShapeDtypeStruct((owned, HD), bf16),
            jax.ShapeDtypeStruct((owned, HD), bf16),
        ),
        in_specs=[hbm] * 2 + [vmem] * 2 + [hbm] * 2 + [smem] * 2,
        out_specs=(vmem, vmem, vmem),
        scratch_shapes=[
            pltpu.VMEM((ROWS, HEADS * HD), bf16),
            pltpu.VMEM((ROWS, HEADS * HD), bf16),
            pltpu.VMEM((KEYS, HD), bf16),
            pltpu.VMEM((KEYS, HD), bf16),
            pltpu.VMEM((2, 4, 4, DO + SLOT, HD), bf16),
            pltpu.VMEM((KEYS, HD), bf16),
            pltpu.VMEM((HD, KEYS), bf16),
            pltpu.VMEM((KEYS, HD), f32),
            pltpu.VMEM((KEYS, HD), f32),
            pltpu.VMEM((HD, 32 * SLOT), f32),
            pltpu.VMEM((2, 3, 4, HD, SLOT), bf16),
            pltpu.VMEM((2, 3, 4, HD, SLOT), bf16),
            pltpu.VMEM((6, HD, SLOT), bf16),
            pltpu.VMEM((6, HD, SLOT), bf16),
            pltpu.VMEM((HD, SLOT), bf16),
            pltpu.VMEM((HD, SLOT), bf16),
            pltpu.VMEM((4, TILE, HD), bf16),
            pltpu.VMEM((4, TILE, HD), bf16),
            pltpu.VMEM((3 * TILE, HD), bf16),
            pltpu.VMEM((3 * TILE, HD), bf16),
            dma((15,)), dma((25,)), dma((13,)), dma((6,)), dma((6,)),
            dma((19,)), dma((19,)), dma((4,)), dma((4,)), dma((7,)), dma((7,)),
            pltpu.SemaphoreType.REGULAR, pltpu.SemaphoreType.REGULAR,
        ],
        compiler_params=pltpu.CompilerParams(
            collective_id=0, has_side_effects=True, vmem_limit_bytes=64 * 1024 * 1024),
    )(queries[0], grad_out[0], row_lse[0].T, row_delta[0].T, prefix_keys, prefix_values, resp_len, visible)


def solution(mesh):
    in_specs = (
        P("resp", "seq", None),
        P("resp", "seq", None),
        P("resp", "seq", None),
        P("resp", "seq", None),
        P("seq", None),
        P("seq", None),
        P("resp"),
        P("resp"),
    )
    out_specs = (P("resp", "seq", None), P(("seq", "resp"), None), P(("seq", "resp"), None))
    return jax.shard_map(
        on_device, mesh=mesh, in_specs=in_specs, out_specs=out_specs, check_vma=False
    )
```
